32 devices in a mesh: region: 2 (over core), shard: 16 (over z, y, x).
Axes of the slice: x: 2, y: 2, z: 4, core: 2. Of those that a mesh axis runs over, the one named last changes fastest.
Arguments:
- points: bfloat16 [3072, 8, 128], P(('region', 'shard')), may hold values from -12 to 12
- block_owner: int32 [3072, 1], P(('region', 'shard')), may hold values from 0 to 15; in each aligned block of 96 rows (0 to 95, 96 to 191, ...) at most 12 rows name the same one
- block_node: int32 [3072], P(('region', 'shard')), may hold values from 0 to 1
- queries: bfloat16 [8192, 128], P(('region', 'shard')), may hold values from -240 to 240
- w_in: bfloat16 [128, 768], replicated, may hold values from -0.5 to 0.5
- w_key: bfloat16 [768, 768], replicated, may hold values from -0.21875 to 0.21875
- w_value: bfloat16 [768, 768], replicated, may hold values from -0.21875 to 0.21875
- w_query: bfloat16 [128, 768], replicated, may hold values from -0.5 to 0.5
- w_out: bfloat16 [768, 128], replicated, may hold values from -0.21875 to 0.21875
Outputs:
- readout: bfloat16 [8192, 128], P(('region', 'shard'))
The draws below stay inside these ranges and needn't reach their ends.
Inputs may be any that keep to these rules, and one draw needn't show every extreme that they name: `block_owner`: among the 96 blocks of one device no shard is named more than 12 times, and some device names one shard exactly 12 times.
All inputs are finite; a program needn't handle non-finite values.
Results may differ from the reference program's by a relative error of at most 0.018.
Values may be sent and summed in bfloat16 or wider, within the bound.
A program may use at most 64 MiB of HBM per device.

```python
import math
import jax
import jax.numpy as jnp
import numpy as np
from jax import lax

D = 768
HEADS = 12
HEAD_DIM = 64
C_IN = 128
C_OUT = 128
BLK = 8
NB = 96
S_DEV = 2
Q_DEV = 256
SHARDS = 16
CAP = 12
BLOCKS = 3072
ANCHORS = 64
QUERIES = 8192


def draw_points(key, part):
    base = jax.random.fold_in(key, 11)
    centre = jax.random.normal(jax.random.fold_in(base, 1), (BLOCKS, 1, C_IN), jnp.float32)
    jitter = jax.random.normal(jax.random.fold_in(base, 2), (BLOCKS, BLK, C_IN), jnp.float32)
    values = 1.5 * centre + 0.6 * jitter
    return jnp.clip(values, -12.0, 12.0).astype(jnp.bfloat16)


def draw_queries(key, part):
    base = jax.random.fold_in(key, 23)
    raw = jax.random.normal(jax.random.fold_in(base, 1), (QUERIES, C_IN), jnp.float32)
    values = raw
    return jnp.clip(values, -240.0, 240.0).astype(jnp.bfloat16)


def with_ends(entries, own_key, smallest, top_value):
    longest = entries.shape.index(max(entries.shape))
    spots = []
    for shift in (0, 1):
        where = [jax.random.randint(jax.random.fold_in(own_key, axis), (), 0, length) for axis, length in enumerate(entries.shape)]
        where[longest] = (where[longest] + shift) % entries.shape[longest]
        spots.append(tuple(where))
    return entries.at[spots[0]].set(smallest).at[spots[1]].set(top_value)


def deal_out(own_key, own, number, rows, amount, top, bound, skew):
    ranking = jax.random.permutation(own_key, amount)
    heavy_load, usual = shares(amount, rows * top, bound, skew, True), shares(amount, rows * top, bound, skew, False)
    places = jnp.arange(amount)

    def named(sizes, offset_by):
        used = int((sizes > 0).sum())
        fixed = max(1, used // 4)
        moved = fixed + (places - fixed + offset_by * (used - fixed)) % max(1, amount - fixed)
        return jnp.zeros((amount,), jnp.int32).at[ranking[jnp.where(places < fixed, places, moved)]].set(jnp.asarray(sizes, jnp.int32))

    sizes = jnp.where(number % 4 == 0, named(heavy_load, number // 4), named(usual, number - number // 4 - 1))
    mixed = jax.random.permutation(jax.random.fold_in(own, 3), amount)
    donor, receiver = mixed[0:amount // 2 * 2:2], mixed[1:amount // 2 * 2:2]
    slack = jnp.minimum(sizes[donor] - 1, bound - sizes[receiver]) // 2
    slack = jnp.where((donor == ranking[0]) | (receiver == ranking[0]) | (sizes[receiver] == 0), 0, jnp.maximum(slack, 0))
    moved = jax.random.randint(jax.random.fold_in(own, 4), (amount // 2,), 0, 1 << 20) % (slack + 1)
    sizes = sizes.at[donor].add(-moved).at[receiver].add(moved)
    labels = jnp.searchsorted(jnp.cumsum(sizes), jnp.arange(rows * top), side="right").astype(jnp.int32)
    grid = labels.reshape(top, rows).T
    grid = grid[jax.random.permutation(jax.random.fold_in(own, 1), rows)]
    offset_by = jax.random.randint(jax.random.fold_in(own, 2), (rows, 1), 0, top)
    return jnp.take_along_axis(grid, (jnp.arange(top)[None, :] + offset_by) % top, axis=1)


def shares(count, total, reach, skew, full):
    weights = [(1 << 20) // math.isqrt(standing ** skew) + 1 for standing in range(1, count + 1)]
    largest = reach if full else min(reach, max(-(-total // count), total * weights[0] // sum(weights)))
    least = 1 if total - largest >= count - 1 else 0
    counts, rest = [largest] + [least] * (count - 1), total - largest - least * (count - 1)
    while rest > 0:
        free = [i for i in range(1, count) if counts[i] < largest] or [i for i in range(1, count) if counts[i] < reach]
        pool, remaining = sum([weights[i] for i in free]), rest
        for i in free:
            more = min(reach - counts[i], max(1, remaining * weights[i] // pool), rest)
            counts[i] = counts[i] + more
            rest = rest - more
    return np.array(counts)


def noise(rng, extent, scale, most, kind=jnp.bfloat16):
    return jnp.clip(scale * jax.random.normal(rng, extent, jnp.float32), -most, most).astype(kind)


def setup_inputs(seed: int = 0) -> dict:
    arg_keys = jax.random.split(jax.random.key(seed), 10)
    points = draw_points(jax.random.fold_in(arg_keys[9], 71), 0)
    block_owner_keys = jax.random.split(jax.random.fold_in(arg_keys[1], 1), BLOCKS // NB)
    block_owner_turns = jax.random.permutation(jax.random.fold_in(arg_keys[1], 3), BLOCKS // NB)
    block_owner = jax.vmap(lambda own, number: deal_out(jax.random.fold_in(arg_keys[1], 2), own, number, NB, SHARDS, 1, CAP, 2))(block_owner_keys, block_owner_turns).reshape((BLOCKS, 1))
    block_node = with_ends(jax.random.randint(arg_keys[2], (BLOCKS,), 0, S_DEV), jax.random.fold_in(arg_keys[2], 1), 0, S_DEV - 1).astype(jnp.int32)
    queries = draw_queries(jax.random.fold_in(arg_keys[9], 71), 0)
    w_in = noise(arg_keys[4], (C_IN, D), C_IN ** -0.5, 0.5)
    w_key = noise(arg_keys[5], (D, D), D ** -0.5, 0.21875)
    w_value = noise(arg_keys[6], (D, D), D ** -0.5, 0.21875)
    w_query = noise(arg_keys[7], (C_IN, D), C_IN ** -0.5, 0.5)
    w_out = noise(arg_keys[8], (D, C_OUT), D ** -0.5, 0.21875)
    return {"points": points, "block_owner": block_owner, "block_node": block_node, "queries": queries, "w_in": w_in, "w_key": w_key, "w_value": w_value, "w_query": w_query, "w_out": w_out}


def layer_norm(pooled):
    mean = lax.optimization_barrier(jnp.mean(pooled, axis=-1, keepdims=True))
    centred = pooled - mean
    spread = lax.optimization_barrier(jnp.mean(centred * centred, axis=-1, keepdims=True))
    return (centred * lax.rsqrt(spread + 1e-05)).astype(jnp.bfloat16)

def reference(points, block_owner, block_node, queries, w_in, w_key, w_value, w_query, w_out):
    device_count = BLOCKS // NB
    region_of = jnp.arange(device_count, dtype=jnp.int32) // SHARDS
    grouped = points.reshape(device_count, NB, BLK, C_IN)
    owner_shard = block_owner[:, 0].reshape(device_count, NB)
    node_ids = ((region_of[:, None] * SHARDS + owner_shard) * S_DEV + block_node.reshape(device_count, NB)).astype(jnp.int32)

    def add_device(pooled, item):
        block_points, block_nodes = item
        message = jax.nn.gelu(jnp.einsum('bpc,cd->bpd', block_points.astype(jnp.float32), w_in.astype(jnp.float32))).astype(jnp.bfloat16)
        block_total = lax.optimization_barrier(jnp.sum(message.astype(jnp.float32), axis=1))
        return (pooled + jax.ops.segment_sum(block_total, block_nodes, num_segments=ANCHORS), None)
    pooled, unused = lax.scan(add_device, jnp.zeros((ANCHORS, D), jnp.float32), (grouped, node_ids))
    normed = layer_norm(pooled)
    keys = jnp.dot(normed, w_key, preferred_element_type=jnp.float32).astype(jnp.bfloat16)
    values = jnp.dot(normed, w_value, preferred_element_type=jnp.float32).astype(jnp.bfloat16)
    key_heads = keys.reshape(ANCHORS, HEADS, HEAD_DIM).astype(jnp.float32)
    value_heads = values.reshape(ANCHORS, HEADS, HEAD_DIM).astype(jnp.float32)
    score_scale = HEAD_DIM ** (-0.5)

    def attend_block(query_rows):
        query_vec = jnp.dot(query_rows, w_query, preferred_element_type=jnp.float32).astype(jnp.bfloat16)
        query_heads = query_vec.reshape(query_rows.shape[0], HEADS, HEAD_DIM).astype(jnp.float32)
        scores = jnp.einsum('qhd,ahd->qha', query_heads, key_heads) * score_scale
        expo = jnp.exp(scores - lax.optimization_barrier(jnp.max(scores, axis=-1, keepdims=True)))
        totals = lax.optimization_barrier(jnp.sum(expo, axis=-1))
        weights = expo.astype(jnp.bfloat16)
        summed = jnp.einsum('qha,ahd->qhd', weights.astype(jnp.float32), value_heads)
        attended = (summed / totals[..., None]).astype(jnp.bfloat16).reshape(query_rows.shape[0], D)
        return jnp.dot(attended, w_out, preferred_element_type=jnp.float32).astype(jnp.bfloat16)
    blocks_out = lax.map(attend_block, queries.reshape(device_count, Q_DEV, C_IN))
    return blocks_out.reshape(QUERIES, C_OUT)
```

```python
import functools

import jax
import jax.numpy as jnp
from jax import lax
from jax.experimental import pallas as pl
from jax.experimental.pallas import tpu as pltpu
from jax.sharding import PartitionSpec as P

HEADS = 12
HEAD_DIM = 64
S_DEV = 2
LANES = 128
ROWS = 16
MESH = pl.DeviceIdType.MESH
F32 = jnp.float32
BF16 = jnp.bfloat16


def dot(a, b, dims=((1,), (0,))):
    return lax.dot_general(a, b, (dims, ((), ())), preferred_element_type=F32)


def iota(shape, axis):
    return lax.broadcasted_iota(jnp.int32, shape, axis)


def each(count, do):
    if count <= 32:
        for k in range(count):
            do(k)
    else:
        lax.fori_loop(0, count, lambda k, c: (do(k), c)[1], 0)


def kernel(
    regions, shards,
    points_hbm, owner_ref, node_ref, queries_hbm, w_in_hbm, w_key_hbm, w_value_hbm, w_query_hbm, w_out_hbm,
    out_ref,
    points, queries, w_in, w_key, w_value, w_query, w_out,
    send1, recv1, send2, recv2, query_t, fold, in_sem, send1_sem, recv1_sem, send2_sem, recv2_sem,
):
    devices = regions * shards
    point_rows, _ = points.shape
    width = w_in.shape[1]
    chunks = width // LANES
    blocks = owner_ref.shape[1]
    region = lax.axis_index("region")
    shard = lax.axis_index("shard")
    me = region * shards + shard

    barrier = pltpu.get_barrier_semaphore()

    def peer(k):
        other = lax.rem(me + k + 1, devices)
        return (other // shards, lax.rem(other, shards))

    loads = [
        pltpu.make_async_copy(src, dst, in_sem.at[k])
        for k, (src, dst) in enumerate((
            (points_hbm, points), (w_in_hbm, w_in), (queries_hbm, queries), (w_query_hbm, w_query),
            (w_out_hbm, w_out), (w_value_hbm, w_value), (w_key_hbm, w_key),
        ))
    ]
    for load in loads:
        load.start()

    def greet(k):
        pl.semaphore_signal(barrier, inc=1, device_id=peer(k), device_id_type=MESH)

    each(devices - 1, greet)

    ids = owner_ref[...] * S_DEV + node_ref[...]
    assign = (iota((S_DEV * shards, blocks), 0) == ids).astype(BF16)
    per_block = point_rows // blocks
    expand = (iota((blocks, point_rows), 1) // per_block == iota((blocks, point_rows), 0)).astype(BF16)
    assign = dot(assign, expand).astype(BF16)

    loads[0].wait()
    loads[1].wait()
    message = jax.nn.gelu(dot(points[...], w_in[...])).astype(BF16)
    partial = dot(assign, message).astype(BF16)
    stacked = jnp.concatenate([partial[:, j * LANES:(j + 1) * LANES] for j in range(chunks)], axis=0)
    place_shape = (shards * ROWS, chunks * S_DEV * shards)
    row, col = iota(place_shape, 0), iota(place_shape, 1)
    inner = row % ROWS
    wanted = (inner // S_DEV) * (S_DEV * shards) + (row // ROWS) * S_DEV + inner % S_DEV
    place = ((wanted == col) & (inner < chunks * S_DEV)).astype(BF16)
    send1[...] = dot(place, stacked).astype(BF16)

    pl.semaphore_wait(barrier, devices - 1)

    def tile(index):
        return pl.ds(pl.multiple_of(index * ROWS, ROWS), ROWS)

    own1 = pltpu.make_async_copy(send1.at[tile(shard)], recv1.at[tile(shard)], recv1_sem)
    own1.start()

    def scatter(k):
        to = lax.rem(shard + k + 1, shards)
        pltpu.make_async_remote_copy(
            src_ref=send1.at[tile(to)], dst_ref=recv1.at[tile(shard)],
            send_sem=send1_sem, recv_sem=recv1_sem, device_id=(region, to), device_id_type=MESH,
        ).start()

    each(shards - 1, scatter)

    loads[2].wait()
    loads[3].wait()
    query_t[...] = (dot(w_query[...], queries[...], ((0,), (1,))) * HEAD_DIM ** (-0.5)).astype(BF16)
    loads[4].wait()
    loads[5].wait()

    def fold_heads():
        for h in range(HEADS):
            head = slice(h * HEAD_DIM, (h + 1) * HEAD_DIM)
            fold[:, h * LANES:(h + 1) * LANES] = dot(w_value[:, head], w_out[head, :]).astype(BF16)

    fold_heads()

    pltpu.make_async_copy(recv1, recv1, recv1_sem).wait()
    total = recv1[0:ROWS, :].astype(F32)
    for s in range(1, shards):
        total = total + recv1[s * ROWS:(s + 1) * ROWS, :].astype(F32)

    inner = iota((ROWS, LANES), 0)
    real = inner < chunks * S_DEV

    def node_mean(x):
        sums = jnp.sum(x, axis=1, keepdims=True)
        which = iota((ROWS, 1), 0) % S_DEV
        mean = jnp.zeros((ROWS, 1), F32)
        for i in range(S_DEV):
            part = jnp.sum(jnp.where(which == i, sums, 0.0), axis=0, keepdims=True)
            mean = jnp.where(which == i, part, mean)
        return mean * (1.0 / width)

    centred = jnp.where(real, total - node_mean(total), 0.0)
    spread = node_mean(centred * centred)
    send2[...] = (centred * lax.rsqrt(spread + 1e-05)).astype(BF16)

    own2 = pltpu.make_async_copy(send2, recv2.at[tile(me)], recv2_sem)
    own2.start()

    def spread_out(k):
        pltpu.make_async_remote_copy(
            src_ref=send2, dst_ref=recv2.at[tile(me)],
            send_sem=send2_sem, recv_sem=recv2_sem, device_id=peer(k), device_id_type=MESH,
        ).start()

    each(devices - 1, spread_out)

    group_devices = LANES // 2 // S_DEV
    anchors = group_devices * S_DEV
    heads_of = 256 // HEAD_DIM
    pick_shape = (chunks * anchors, group_devices * ROWS)
    row, col = iota(pick_shape, 0), iota(pick_shape, 1)
    anchor = row % anchors
    pick = ((anchor // S_DEV) * ROWS + (row // anchors) * S_DEV + anchor % S_DEV == col).astype(BF16)
    diag_shape = (heads_of * anchors, heads_of * HEAD_DIM)
    diagonal = iota(diag_shape, 0) // anchors == iota(diag_shape, 1) // HEAD_DIM
    loads[6].wait()

    pltpu.make_async_copy(recv2, recv2, recv2_sem).wait()
    keys, folded = [], []
    for c in range(devices // group_devices):
        rows = recv2[c * group_devices * ROWS:(c + 1) * group_devices * ROWS, :]
        picked = dot(pick, rows).astype(BF16)
        normed = jnp.concatenate([picked[j * anchors:(j + 1) * anchors] for j in range(chunks)], axis=1)
        keys.append(dot(normed, w_key[...]).astype(BF16))
        folded.append(dot(normed, fold[...]))

    readout_t = jnp.zeros((LANES, queries.shape[0]), F32)
    for g in range(HEADS // heads_of):
        features = slice(g * 256, (g + 1) * 256)
        scores = []
        for key in keys:
            block = jnp.where(diagonal, jnp.concatenate([key[:, features]] * heads_of, axis=0), jnp.zeros((), BF16))
            scores.append(dot(block, query_t[features, :]))
        expos = [[] for _ in keys]
        for h in range(heads_of):
            head = [s[h * anchors:(h + 1) * anchors] for s in scores]
            peak = functools.reduce(jnp.maximum, [jnp.max(s, axis=0, keepdims=True) for s in head])
            expo = [jnp.exp(s - peak) for s in head]
            scale = 1.0 / sum(jnp.sum(e, axis=0, keepdims=True) for e in expo)
            for c, e in enumerate(expo):
                expos[c].append((e * scale).astype(BF16))
        for c, value in enumerate(folded):
            weights = jnp.concatenate(expos[c], axis=0)
            value = jnp.concatenate(
                [value[:, h * LANES:(h + 1) * LANES] for h in range(g * heads_of, (g + 1) * heads_of)], axis=0
            )
            readout_t = readout_t + dot(value.T.astype(BF16), weights)
    out_ref[...] = readout_t.T.astype(BF16)

    sent1 = send1.at[pl.ds(0, (shards - 1) * ROWS)]
    pltpu.make_async_copy(sent1, sent1, send1_sem).wait()
    sent2 = recv2.at[pl.ds(0, (devices - 1) * ROWS)]
    pltpu.make_async_copy(sent2, sent2, send2_sem).wait()


def body(regions, shards, points, block_owner, block_node, queries, w_in, w_key, w_value, w_query, w_out):
    blocks, per_block, features = points.shape
    points = points.reshape(blocks * per_block, features)
    owner = block_owner.reshape(1, blocks)
    node = block_node.reshape(1, blocks)
    width = w_in.shape[1]
    hbm = pl.BlockSpec(memory_space=pl.ANY)
    vmem = pl.BlockSpec(memory_space=pltpu.VMEM)
    devices = regions * shards
    local = [points, queries, w_in, w_key, w_value, w_query, w_out]
    return pl.pallas_call(
        functools.partial(kernel, regions, shards),
        out_shape=jax.ShapeDtypeStruct((queries.shape[0], w_out.shape[1]), BF16),
        in_specs=[hbm, vmem, vmem] + [hbm] * 6,
        out_specs=vmem,
        scratch_shapes=[pltpu.VMEM(x.shape, x.dtype) for x in local] + [
            pltpu.VMEM((shards * ROWS, LANES), BF16),
            pltpu.VMEM((shards * ROWS, LANES), BF16),
            pltpu.VMEM((ROWS, LANES), BF16),
            pltpu.VMEM((devices * ROWS, LANES), BF16),
            pltpu.VMEM((width, queries.shape[0]), BF16),
            pltpu.VMEM((width, HEADS * LANES), BF16),
            pltpu.SemaphoreType.DMA((7,)),
            pltpu.SemaphoreType.DMA,
            pltpu.SemaphoreType.DMA,
            pltpu.SemaphoreType.DMA,
            pltpu.SemaphoreType.DMA,
        ],
        compiler_params=pltpu.CompilerParams(
            collective_id=0, has_side_effects=True, vmem_limit_bytes=48 * 1024 * 1024
        ),
    )(points, owner, node, queries, w_in, w_key, w_value, w_query, w_out)


def solution(mesh):
    both = ("region", "shard")
    return jax.shard_map(
        functools.partial(body, mesh.shape["region"], mesh.shape["shard"]),
        mesh=mesh,
        in_specs=(P(both, None, None), P(both, None), P(both), P(both, None), P(), P(), P(), P(), P()),
        out_specs=P(both, None),
        check_vma=False,
    )
```

```python
import functools

import jax
import jax.numpy as jnp
from jax import lax
from jax.experimental import pallas as pl
from jax.experimental.pallas import tpu as pltpu
from jax.sharding import PartitionSpec as P

HEADS = 12
HEAD_DIM = 64
S_DEV = 2
LANES = 128
ROWS = 16
VMEM_BYTES = 64 * 1024 * 1024 - 96 * 1024
MESH = pl.DeviceIdType.MESH
F32 = jnp.float32
BF16 = jnp.bfloat16


def dot(a, b, dims=((1,), (0,))):
    return lax.dot_general(a, b, (dims, ((), ())), preferred_element_type=F32)


def iota(shape, axis):
    return lax.broadcasted_iota(jnp.int32, shape, axis)


def selection(rows, cols, wanted, real=None):
    row = iota((rows, LANES), 0)
    lane = iota((rows, LANES), 1)
    column = wanted(row)
    if real is not None:
        column = jnp.where(real(row), column, -1)
    parts = [(column == lane + start).astype(BF16) for start in range(0, cols, LANES)]
    return jnp.concatenate(parts, axis=1)[:, :cols]


def div(x, by):
    return lax.shift_right_logical(x, by.bit_length() - 1) if by & (by - 1) == 0 else x // by


def mod(x, by):
    return x & (by - 1) if by & (by - 1) == 0 else x % by


def each(count, do):
    if count <= 32:
        for k in range(count):
            do(k)
    else:
        lax.fori_loop(0, count, lambda k, c: (do(k), c)[1], 0)


def kernel(
    regions, shards,
    points_hbm, owner_hbm, node_hbm, queries_hbm, w_in_hbm, w_key_hbm, w_value_hbm, w_query_hbm, w_out_hbm,
    out_ref,
    points, owner_ref, node_ref, queries, w_in, w_key, w_value, w_query, w_out,
    send1, recv1, send2, recv2, recv3, query_t, fold, in_sem, send1_sem, recv1_sem, send2_sem, recv2_sem, send3_sem, recv3_sem,
):
    devices = regions * shards
    point_rows, _ = points.shape
    width = w_in.shape[1]
    chunks = width // LANES
    blocks = owner_ref.shape[1]
    region = lax.axis_index("region")
    shard = lax.axis_index("shard")
    me = region * shards + shard

    barrier = pltpu.get_barrier_semaphore()

    def peer(k):
        other = lax.rem(me + k + 1, devices)
        return (other // shards, lax.rem(other, shards))

    loads = [
        pltpu.make_async_copy(src, dst, in_sem.at[k])
        for k, (src, dst) in enumerate((
            (points_hbm, points), (w_in_hbm, w_in), (queries_hbm, queries), (w_query_hbm, w_query),
            (w_out_hbm, w_out), (w_value_hbm, w_value), (w_key_hbm, w_key), (owner_hbm, owner_ref), (node_hbm, node_ref),
        ))
    ]
    for load in loads:
        load.start()

    def greet(k):
        pl.semaphore_signal(barrier, inc=1, device_id=peer(k), device_id_type=MESH)

    each(devices - 1, greet)

    loads[7].wait()
    loads[8].wait()
    ids = owner_ref[...] * S_DEV + node_ref[...]
    assign = (iota((S_DEV * shards, blocks), 0) == ids).astype(BF16)
    per_block = point_rows // blocks
    expand = (div(iota((blocks, point_rows), 1), per_block) == iota((blocks, point_rows), 0)).astype(BF16)
    assign = dot(assign, expand).astype(BF16)

    loads[0].wait()
    loads[1].wait()
    message = jax.nn.gelu(dot(points[...], w_in[...])).astype(BF16)
    partial = dot(assign, message).astype(BF16)
    stacked = jnp.concatenate([partial[:, j * LANES:(j + 1) * LANES] for j in range(chunks)], axis=0)
    place = selection(
        shards * ROWS, chunks * S_DEV * shards,
        lambda row: div(mod(row, ROWS), S_DEV) * (S_DEV * shards) + div(row, ROWS) * S_DEV + mod(row, S_DEV),
        lambda row: mod(row, ROWS) < chunks * S_DEV,
    )
    send1[...] = dot(place, stacked).astype(BF16)

    pl.semaphore_wait(barrier, devices - 1)

    def tile(index):
        return pl.ds(pl.multiple_of(index * ROWS, ROWS), ROWS)

    own1 = pltpu.make_async_copy(send1.at[tile(shard)], recv1.at[tile(shard)], recv1_sem)
    own1.start()

    def scatter(k):
        to = lax.rem(shard + k + 1, shards)
        pltpu.make_async_remote_copy(
            src_ref=send1.at[tile(to)], dst_ref=recv1.at[tile(shard)],
            send_sem=send1_sem, recv_sem=recv1_sem, device_id=(region, to), device_id_type=MESH,
        ).start()

    each(shards - 1, scatter)

    loads[2].wait()
    loads[3].wait()
    query_t[...] = (dot(w_query[...], queries[...], ((0,), (1,))) * HEAD_DIM ** (-0.5)).astype(BF16)
    group_devices = ROWS
    anchors = group_devices * S_DEV
    heads_of = 256 // HEAD_DIM
    pick = selection(
        chunks * anchors, group_devices * ROWS,
        lambda row: div(mod(row, anchors), S_DEV) * ROWS + div(row, anchors) * S_DEV + mod(row, S_DEV),
    )
    diag_shape = (heads_of * anchors, heads_of * HEAD_DIM)
    diagonal = div(iota(diag_shape, 0), anchors) == div(iota(diag_shape, 1), HEAD_DIM)
    pltpu.make_async_copy(recv1, recv1, recv1_sem).wait()
    total = recv1[0:ROWS, :].astype(F32)
    for s in range(1, shards):
        total = total + recv1[s * ROWS:(s + 1) * ROWS, :].astype(F32)

    inner = iota((ROWS, LANES), 0)
    real = inner < chunks * S_DEV

    def node_mean(x):
        sums = jnp.sum(x, axis=1, keepdims=True)
        which = mod(iota((ROWS, 1), 0), S_DEV)
        mean = jnp.zeros((ROWS, 1), F32)
        for i in range(S_DEV):
            part = jnp.sum(jnp.where(which == i, sums, 0.0), axis=0, keepdims=True)
            mean = jnp.where(which == i, part, mean)
        return mean * (1.0 / width)

    centred = jnp.where(real, total - node_mean(total), 0.0)
    spread = node_mean(centred * centred)
    send2[...] = (centred * lax.rsqrt(spread + 1e-05)).astype(BF16)

    own2 = pltpu.make_async_copy(send2, recv2.at[tile(shard)], recv2_sem)
    own2.start()

    def spread_out(k):
        to = lax.rem(shard + k + 1, shards)
        pltpu.make_async_remote_copy(
            src_ref=send2, dst_ref=recv2.at[tile(shard)],
            send_sem=send2_sem, recv_sem=recv2_sem, device_id=(region, to), device_id_type=MESH,
        ).start()

    each(shards - 1, spread_out)

    loads[4].wait()
    loads[5].wait()

    def fold_heads():
        for h in range(HEADS):
            head = slice(h * HEAD_DIM, (h + 1) * HEAD_DIM)
            fold[:, h * LANES:(h + 1) * LANES] = dot(w_value[:, head], w_out[head, :]).astype(BF16)

    fold_heads()

    loads[6].wait()
    pltpu.make_async_copy(recv2, recv2, recv2_sem).wait()

    def pass_on(k):
        slot = pl.ds(k * shards * ROWS, shards * ROWS)
        pltpu.make_async_remote_copy(
            src_ref=recv2, dst_ref=recv3.at[slot],
            send_sem=send3_sem, recv_sem=recv3_sem,
            device_id=(lax.rem(region + k + 1, regions), shard), device_id_type=MESH,
        ).start()

    each(regions - 1, pass_on)

    keys, folded = [], []

    def project(source):
        for start in range(0, source.shape[0], group_devices * ROWS):
            picked = dot(pick, source[start:start + group_devices * ROWS, :]).astype(BF16)
            normed = jnp.concatenate([picked[j * anchors:(j + 1) * anchors] for j in range(chunks)], axis=1)
            keys.append(dot(normed, w_key[...]).astype(BF16))
            folded.append(dot(normed, fold[...]))

    project(recv2)
    pltpu.make_async_copy(recv3, recv3, recv3_sem).wait()
    project(recv3)

    readout_t = jnp.zeros((LANES, queries.shape[0]), F32)
    for g in range(HEADS // heads_of):
        features = slice(g * 256, (g + 1) * 256)
        scores = []
        for key in keys:
            block = jnp.where(diagonal, jnp.concatenate([key[:, features]] * heads_of, axis=0), jnp.zeros((), BF16))
            scores.append(dot(block, query_t[features, :]))
        expos = [[] for _ in keys]
        for h in range(heads_of):
            head = [s[h * anchors:(h + 1) * anchors] for s in scores]
            peak = functools.reduce(jnp.maximum, [jnp.max(s, axis=0, keepdims=True) for s in head])
            expo = [jnp.exp(s - peak) for s in head]
            scale = 1.0 / sum(jnp.sum(e, axis=0, keepdims=True) for e in expo)
            for c, e in enumerate(expo):
                expos[c].append((e * scale).astype(BF16))
        weights = jnp.concatenate([e for part in expos for e in part], axis=0)
        values = jnp.concatenate(
            [value[:, h * LANES:(h + 1) * LANES] for value in folded for h in range(g * heads_of, (g + 1) * heads_of)],
            axis=0,
        )
        readout_t = readout_t + dot(values.T.astype(BF16), weights)
    out_ref[...] = readout_t.T.astype(BF16)

    sent1 = send1.at[pl.ds(0, (shards - 1) * ROWS)]
    pltpu.make_async_copy(sent1, sent1, send1_sem).wait()
    sent2 = recv2.at[pl.ds(0, (shards - 1) * ROWS)]
    pltpu.make_async_copy(sent2, sent2, send2_sem).wait()
    pltpu.make_async_copy(recv3, recv3, send3_sem).wait()


def body(regions, shards, points, block_owner, block_node, queries, w_in, w_key, w_value, w_query, w_out):
    blocks, per_block, features = points.shape
    points = points.reshape(blocks * per_block, features)
    owner = block_owner.reshape(1, blocks)
    node = block_node.reshape(1, blocks)
    width = w_in.shape[1]
    hbm = pl.BlockSpec(memory_space=pltpu.HBM)
    vmem = pl.BlockSpec(memory_space=pltpu.VMEM)
    local = [points, owner, node, queries, w_in, w_key, w_value, w_query, w_out]
    return pl.pallas_call(
        functools.partial(kernel, regions, shards),
        out_shape=jax.ShapeDtypeStruct((queries.shape[0], w_out.shape[1]), BF16),
        in_specs=[hbm] * 9,
        out_specs=vmem,
        scratch_shapes=[pltpu.VMEM(x.shape, x.dtype) for x in local] + [
            pltpu.VMEM((shards * ROWS, LANES), BF16),
            pltpu.VMEM((shards * ROWS, LANES), BF16),
            pltpu.VMEM((ROWS, LANES), BF16),
            pltpu.VMEM((shards * ROWS, LANES), BF16),
            pltpu.VMEM(((regions - 1) * shards * ROWS, LANES), BF16),
            pltpu.VMEM((width, queries.shape[0]), BF16),
            pltpu.VMEM((width, HEADS * LANES), BF16),
            pltpu.SemaphoreType.DMA((9,)),
            pltpu.SemaphoreType.DMA,
            pltpu.SemaphoreType.DMA,
            pltpu.SemaphoreType.DMA,
            pltpu.SemaphoreType.DMA,
            pltpu.SemaphoreType.DMA,
            pltpu.SemaphoreType.DMA,
        ],
        compiler_params=pltpu.CompilerParams(
            collective_id=0, has_side_effects=True, vmem_limit_bytes=VMEM_BYTES
        ),
    )(points, owner, node, queries, w_in, w_key, w_value, w_query, w_out)


def solution(mesh):
    both = ("region", "shard")
    return jax.shard_map(
        functools.partial(body, mesh.shape["region"], mesh.shape["shard"]),
        mesh=mesh,
        in_specs=(P(both, None, None), P(both, None), P(both), P(both, None), P(), P(), P(), P(), P()),
        out_specs=P(both, None),
        check_vma=False,
    )
```

```python
import functools

import jax
import jax.numpy as jnp
from jax import lax
from jax.experimental import pallas as pl
from jax.experimental.pallas import tpu as pltpu
from jax.sharding import PartitionSpec as P

HEADS = 12
HEAD_DIM = 64
S_DEV = 2
LANES = 128
ROWS = 16
VMEM_BYTES = 64 * 1024 * 1024 - 96 * 1024
MESH = pl.DeviceIdType.MESH
F32 = jnp.float32
BF16 = jnp.bfloat16


def dot(a, b, dims=((1,), (0,))):
    return lax.dot_general(a, b, (dims, ((), ())), preferred_element_type=F32)


def iota(shape, axis):
    return lax.broadcasted_iota(jnp.int32, shape, axis)


def selection(rows, cols, wanted, real=None):
    row = iota((rows, LANES), 0)
    lane = iota((rows, LANES), 1)
    column = wanted(row)
    if real is not None:
        column = jnp.where(real(row), column, -1)
    parts = [(column == lane + start).astype(BF16) for start in range(0, cols, LANES)]
    return jnp.concatenate(parts, axis=1)[:, :cols]


def div(x, by):
    return lax.shift_right_logical(x, by.bit_length() - 1) if by & (by - 1) == 0 else x // by


def mod(x, by):
    return x & (by - 1) if by & (by - 1) == 0 else x % by


def each(count, do):
    if count <= 32:
        for k in range(count):
            do(k)
    else:
        lax.fori_loop(0, count, lambda k, c: (do(k), c)[1], 0)


def kernel(
    regions, shards,
    points_hbm, owner_hbm, node_hbm, queries_hbm, w_in_hbm, w_key_hbm, w_value_hbm, w_query_hbm, w_out_hbm,
    out_ref,
    points, owner_ref, node_ref, queries, w_in, w_key, w_value, w_query, w_out,
    send1, recv1, send2, recv2, recv3, query_t, fold, in_sem, send1_sem, recv1_sem, send2_sem, recv2_sem, send3_sem, recv3_sem,
):
    point_rows, _ = points.shape
    width = w_in.shape[1]
    chunks = width // LANES
    blocks = owner_ref.shape[1]
    region = lax.axis_index("region")
    shard = lax.axis_index("shard")

    barrier = pltpu.get_barrier_semaphore()

    loads = [
        pltpu.make_async_copy(src, dst, in_sem.at[k])
        for k, (src, dst) in enumerate((
            (points_hbm, points), (w_in_hbm, w_in), (queries_hbm, queries), (w_query_hbm, w_query),
            (w_out_hbm, w_out), (w_value_hbm, w_value), (w_key_hbm, w_key), (owner_hbm, owner_ref), (node_hbm, node_ref),
        ))
    ]
    for k in (7, 8, 0, 1):
        loads[k].start()

    def greet(k):
        pl.semaphore_signal(
            barrier, inc=1, device_id=(region, mod(shard + k + 1, shards)), device_id_type=MESH
        )

    def greet_region(k):
        pl.semaphore_signal(
            barrier, inc=1, device_id=(mod(region + k + 1, regions), shard), device_id_type=MESH
        )

    each(shards - 1, greet)
    each(regions - 1, greet_region)

    loads[7].wait()
    loads[8].wait()
    ids = owner_ref[...] * S_DEV + node_ref[...]
    assign = (iota((S_DEV * shards, blocks), 0) == ids).astype(BF16)
    per_block = point_rows // blocks
    expand = (div(iota((blocks, point_rows), 1), per_block) == iota((blocks, point_rows), 0)).astype(BF16)
    assign = dot(assign, expand).astype(BF16)

    loads[0].wait()
    loads[1].wait()
    for k in (2, 3, 4, 5, 6):
        loads[k].start()
    message = jax.nn.gelu(dot(points[...], w_in[...]).astype(BF16))
    partial = dot(assign, message).astype(BF16)
    stacked = jnp.concatenate([partial[:, j * LANES:(j + 1) * LANES] for j in range(chunks)], axis=0)
    place = selection(
        shards * ROWS, chunks * S_DEV * shards,
        lambda row: div(mod(row, ROWS), S_DEV) * (S_DEV * shards) + div(row, ROWS) * S_DEV + mod(row, S_DEV),
        lambda row: mod(row, ROWS) < chunks * S_DEV,
    )
    send1[...] = dot(place, stacked).astype(BF16)

    pl.semaphore_wait(barrier, shards + regions - 2)

    def tile(index):
        return pl.ds(pl.multiple_of(index * ROWS, ROWS), ROWS)

    own1 = pltpu.make_async_copy(send1.at[tile(shard)], recv1.at[tile(shard)], recv1_sem)
    own1.start()

    def scatter(k):
        to = mod(shard + k + 1, shards)
        pltpu.make_async_remote_copy(
            src_ref=send1.at[tile(to)], dst_ref=recv1.at[tile(shard)],
            send_sem=send1_sem, recv_sem=recv1_sem, device_id=(region, to), device_id_type=MESH,
        ).start()

    each(shards - 1, scatter)

    loads[2].wait()
    loads[3].wait()
    query_t[...] = (dot(w_query[...], queries[...], ((0,), (1,))) * HEAD_DIM ** (-0.5)).astype(BF16)
    group_devices = ROWS
    anchors = group_devices * S_DEV
    heads_of = 256 // HEAD_DIM
    pick = selection(
        chunks * anchors, group_devices * ROWS,
        lambda row: div(mod(row, anchors), S_DEV) * ROWS + div(row, anchors) * S_DEV + mod(row, S_DEV),
    )
    diag_shape = (heads_of * anchors, heads_of * HEAD_DIM)
    diagonal = div(iota(diag_shape, 0), anchors) == div(iota(diag_shape, 1), HEAD_DIM)
    pltpu.make_async_copy(recv1, recv1, recv1_sem).wait()
    total = recv1[0:ROWS, :].astype(F32)
    for s in range(1, shards):
        total = total + recv1[s * ROWS:(s + 1) * ROWS, :].astype(F32)

    inner = iota((ROWS, LANES), 0)
    real = inner < chunks * S_DEV

    def node_mean(x):
        sums = jnp.sum(x, axis=1, keepdims=True)
        which = mod(iota((ROWS, 1), 0), S_DEV)
        mean = jnp.zeros((ROWS, 1), F32)
        for i in range(S_DEV):
            part = jnp.sum(jnp.where(which == i, sums, 0.0), axis=0, keepdims=True)
            mean = jnp.where(which == i, part, mean)
        return mean * (1.0 / width)

    centred = jnp.where(real, total - node_mean(total), 0.0)
    spread = node_mean(centred * centred)
    send2[...] = (centred * lax.rsqrt(spread + 1e-05)).astype(BF16)

    own2 = pltpu.make_async_copy(send2, recv2.at[tile(shard)], recv2_sem)
    own2.start()

    def spread_out(k):
        to = mod(shard + k + 1, shards)
        pltpu.make_async_remote_copy(
            src_ref=send2, dst_ref=recv2.at[tile(shard)],
            send_sem=send2_sem, recv_sem=recv2_sem, device_id=(region, to), device_id_type=MESH,
        ).start()

    each(shards - 1, spread_out)

    loads[4].wait()
    loads[5].wait()

    def fold_heads():
        for h in range(HEADS):
            head = slice(h * HEAD_DIM, (h + 1) * HEAD_DIM)
            fold[:, h * LANES:(h + 1) * LANES] = dot(w_value[:, head], w_out[head, :]).astype(BF16)

    fold_heads()

    loads[6].wait()
    pltpu.make_async_copy(recv2, recv2, recv2_sem).wait()

    def pass_on(k):
        slot = pl.ds(k * shards * ROWS, shards * ROWS)
        pltpu.make_async_remote_copy(
            src_ref=recv2, dst_ref=recv3.at[slot],
            send_sem=send3_sem, recv_sem=recv3_sem,
            device_id=(mod(region + k + 1, regions), shard), device_id_type=MESH,
        ).start()

    each(regions - 1, pass_on)

    keys, folded = [], []

    def project(source):
        for start in range(0, source.shape[0], group_devices * ROWS):
            picked = dot(pick, source[start:start + group_devices * ROWS, :]).astype(BF16)
            normed = jnp.concatenate([picked[j * anchors:(j + 1) * anchors] for j in range(chunks)], axis=1)
            keys.append(dot(normed, w_key[...]).astype(BF16))
            folded.append(dot(normed, fold[...]))

    project(recv2)
    pltpu.make_async_copy(recv3, recv3, recv3_sem).wait()
    project(recv3)

    readout_t = jnp.zeros((LANES, queries.shape[0]), F32)
    for g in range(HEADS // heads_of):
        features = slice(g * 256, (g + 1) * 256)
        scores = []
        for key in keys:
            block = jnp.where(diagonal, jnp.concatenate([key[:, features]] * heads_of, axis=0), jnp.zeros((), BF16))
            scores.append(dot(block, query_t[features, :]))
        expos = [[] for _ in keys]
        for h in range(heads_of):
            head = [s[h * anchors:(h + 1) * anchors] for s in scores]
            peak = functools.reduce(jnp.maximum, [jnp.max(s, axis=0, keepdims=True) for s in head])
            expo = [jnp.exp(s - peak) for s in head]
            scale = 1.0 / sum(jnp.sum(e, axis=0, keepdims=True) for e in expo)
            for c, e in enumerate(expo):
                expos[c].append((e * scale).astype(BF16))
        weights = jnp.concatenate([e for part in expos for e in part], axis=0)
        values = jnp.concatenate(
            [value[:, h * LANES:(h + 1) * LANES] for value in folded for h in range(g * heads_of, (g + 1) * heads_of)],
            axis=0,
        )
        readout_t = readout_t + dot(values.T.astype(BF16), weights)
    out_ref[...] = readout_t.T.astype(BF16)

    sent1 = send1.at[pl.ds(0, (shards - 1) * ROWS)]
    pltpu.make_async_copy(sent1, sent1, send1_sem).wait()
    sent2 = recv2.at[pl.ds(0, (shards - 1) * ROWS)]
    pltpu.make_async_copy(sent2, sent2, send2_sem).wait()
    pltpu.make_async_copy(recv3, recv3, send3_sem).wait()


def body(regions, shards, points, block_owner, block_node, queries, w_in, w_key, w_value, w_query, w_out):
    blocks, per_block, features = points.shape
    points = points.reshape(blocks * per_block, features)
    owner = block_owner.reshape(1, blocks)
    node = block_node.reshape(1, blocks)
    width = w_in.shape[1]
    hbm = pl.BlockSpec(memory_space=pltpu.HBM)
    vmem = pl.BlockSpec(memory_space=pltpu.VMEM)
    local = [points, owner, node, queries, w_in, w_key, w_value, w_query, w_out]
    return pl.pallas_call(
        functools.partial(kernel, regions, shards),
        out_shape=jax.ShapeDtypeStruct((queries.shape[0], w_out.shape[1]), BF16),
        in_specs=[hbm] * 9,
        out_specs=vmem,
        scratch_shapes=[pltpu.VMEM(x.shape, x.dtype) for x in local] + [
            pltpu.VMEM((shards * ROWS, LANES), BF16),
            pltpu.VMEM((shards * ROWS, LANES), BF16),
            pltpu.VMEM((ROWS, LANES), BF16),
            pltpu.VMEM((shards * ROWS, LANES), BF16),
            pltpu.VMEM(((regions - 1) * shards * ROWS, LANES), BF16),
            pltpu.VMEM((width, queries.shape[0]), BF16),
            pltpu.VMEM((width, HEADS * LANES), BF16),
            pltpu.SemaphoreType.DMA((9,)),
            pltpu.SemaphoreType.DMA,
            pltpu.SemaphoreType.DMA,
            pltpu.SemaphoreType.DMA,
            pltpu.SemaphoreType.DMA,
            pltpu.SemaphoreType.DMA,
            pltpu.SemaphoreType.DMA,
        ],
        compiler_params=pltpu.CompilerParams(
            collective_id=0, has_side_effects=True, vmem_limit_bytes=VMEM_BYTES
        ),
    )(points, owner, node, queries, w_in, w_key, w_value, w_query, w_out)


def solution(mesh):
    both = ("region", "shard")
    return jax.shard_map(
        functools.partial(body, mesh.shape["region"], mesh.shape["shard"]),
        mesh=mesh,
        in_specs=(P(both, None, None), P(both, None), P(both), P(both, None), P(), P(), P(), P(), P()),
        out_specs=P(both, None),
        check_vma=False,
    )
```
